256 devices in a mesh: tok: 32 (over y, z), wi: 2 (over x_lo), wo: 4 (over x_hi, core).
Axes of the slice: x: 4 (x_hi: 2, x_lo: 2; x = x_hi * 2 + x_lo), y: 4, z: 8, core: 2. Of those that a mesh axis runs over, the one named last changes fastest.
Arguments:
- tokens: bfloat16 [128, 8192], P(('tok', 'wo'), 'wi'), may hold values from -6 to 6
- gate_weight: bfloat16 [28672, 8192], P(('tok', 'wo'), 'wi'), may hold values from -0.0625 to 0.0625
- up_weight: bfloat16 [28672, 8192], P(('tok', 'wo'), 'wi'), may hold values from -0.0625 to 0.0625
- down_weight: bfloat16 [28672, 8192], P(('tok', 'wo'), 'wi'), may hold values from -0.03125 to 0.03125
- cotangent: bfloat16 [128, 8192], P(('tok', 'wo'), 'wi'), may hold values from -6 to 6
Outputs:
- output: bfloat16 [128, 8192], P(('tok', 'wo'), 'wi')
- grad_input: bfloat16 [128, 8192], P(('tok', 'wo'), 'wi')
- grad_gate: bfloat16 [28672, 8192], P(('tok', 'wo'), 'wi')
- grad_up: bfloat16 [28672, 8192], P(('tok', 'wo'), 'wi')
- grad_down: bfloat16 [28672, 8192], P(('tok', 'wo'), 'wi')
The draws below stay inside these ranges and needn't reach their ends.
All inputs are finite; a program needn't handle non-finite values.
Results may differ from the reference program's by a relative error of at most 0.02.
Values may be sent and summed in bfloat16 or wider, within the bound.
A program may use at most 64 MiB of HBM per device.

```python
import jax
import jax.numpy as jnp

D = 8192
FF = 28672
TOKENS = 128


def block_levels(stream_key, extent, split, smallest, top_value):
    def one(axis_at, shards_of):
        steps = jax.random.uniform(jax.random.fold_in(jax.random.fold_in(stream_key, 6), axis_at), (shards_of,), jnp.float32, smallest / len(split), top_value / len(split))
        return jnp.repeat(jnp.exp(steps), extent[axis_at] // shards_of).reshape((-1,) + (1,) * (len(extent) - axis_at - 1))

    factor_of = one(*split[0])
    for cut in split[1:]:
        factor_of = factor_of * one(*cut)
    return factor_of


def scatter_about(own_key, shape, deviation, reach, split=(), held_as=jnp.bfloat16):
    entries = jax.random.normal(own_key, shape, jnp.float32) * deviation
    if len(split) > 0:
        entries = block_levels(own_key, shape, split, -0.22, 0.18) * entries
    return jnp.clip(entries, min=-reach, max=reach).astype(held_as)


def setup_inputs(seed: int = 0) -> dict:
    arg_keys = jax.random.split(jax.random.key(seed), 6)
    tokens = scatter_about(arg_keys[0], (TOKENS, D), 1.0, 6.0, ((0, 128), (1, 2)))
    gate_weight = scatter_about(arg_keys[1], (FF, D), D ** -0.5, 0.0625, ((0, 128), (1, 2)))
    up_weight = scatter_about(arg_keys[2], (FF, D), D ** -0.5, 0.0625, ((0, 128), (1, 2)))
    down_weight = scatter_about(arg_keys[3], (FF, D), FF ** -0.5, 0.03125, ((0, 128), (1, 2)))
    cotangent = scatter_about(arg_keys[4], (TOKENS, D), 1.0, 6.0, ((0, 128), (1, 2)))
    return {"tokens": tokens, "gate_weight": gate_weight, "up_weight": up_weight, "down_weight": down_weight, "cotangent": cotangent}


def reference(tokens, gate_weight, up_weight, down_weight, cotangent):
    gate = jnp.dot(tokens, gate_weight.T, preferred_element_type=jnp.float32)
    up = jnp.dot(tokens, up_weight.T, preferred_element_type=jnp.float32)
    sig = jax.nn.sigmoid(gate)
    act = gate * sig
    hidden = (act * up).astype(jnp.bfloat16)
    output = jnp.dot(hidden, down_weight, preferred_element_type=jnp.float32).astype(jnp.bfloat16)
    dhid = jnp.dot(cotangent, down_weight.T, preferred_element_type=jnp.float32)
    dgate = (dhid * up * sig * (1.0 + gate * (1.0 - sig))).astype(jnp.bfloat16)
    dup = (dhid * act).astype(jnp.bfloat16)
    grad_down = jnp.dot(hidden.T, cotangent, preferred_element_type=jnp.float32).astype(jnp.bfloat16)
    grad_gate = jnp.dot(dgate.T, tokens, preferred_element_type=jnp.float32).astype(jnp.bfloat16)
    grad_up = jnp.dot(dup.T, tokens, preferred_element_type=jnp.float32).astype(jnp.bfloat16)
    back_gate = jnp.dot(dgate, gate_weight, preferred_element_type=jnp.float32)
    back_up = jnp.dot(dup, up_weight, preferred_element_type=jnp.float32)
    grad_input = (back_gate + back_up).astype(jnp.bfloat16)
    return output, grad_input, grad_gate, grad_up, grad_down
```

```python
import functools

import jax
import jax.numpy as jnp
from jax import lax
from jax.experimental import pallas as pl
from jax.experimental.pallas import tpu as pltpu
from jax.sharding import PartitionSpec as P

MESH = pl.DeviceIdType.MESH
BF = jnp.bfloat16
F32 = jnp.float32
NY, NZ, NX, NC = 4, 8, 2, 2
ROW = NZ * NX
HALF = NY * ROW


def nt(left, right):
    return lax.dot_general(left, right, (((1,), (1,)), ((), ())), preferred_element_type=F32)


def nn(left, right):
    return jnp.dot(left, right, preferred_element_type=F32)


def exchange_kernel(
    tok_ref, cot_ref, gw_hbm, uw_hbm, dw_hbm,
    all_out, act_out, rows_out,
    wv, own32, own, zxb, whole, wis, wir, tp, cs, cr, mine, ys, yr, zs, zr, acts,
    w_sem, zx_s, zx_r, y_s, y_r, sib_s, sib_r, wi_s, wi_r,
    c_s, c_r, ry_s, ry_r, rz_s, rz_r, out_sem,
):
    width = wv.shape[2]
    parts = width // (ROW * 128)
    wide = ROW * 128
    tok_i, wi_i, wo_i = lax.axis_index("tok"), lax.axis_index("wi"), lax.axis_index("wo")
    y, z = tok_i // NZ, lax.rem(tok_i, NZ)
    xh, c = wo_i // NC, lax.rem(wo_i, NC)
    zx = z * NX + xh

    def zx_dev(d):
        t = lax.rem(zx + d, ROW)
        return (y * NZ + t // NX, wi_i, lax.rem(t, NX) * NC + c), t

    def y_dev(d):
        t = lax.rem(y + d, NY)
        return (t * NZ + z, wi_i, wo_i), t

    sib = (tok_i, wi_i, xh * NC + (1 - c))
    pair = (tok_i, 1 - wi_i, wo_i)

    barrier = pltpu.get_barrier_semaphore()

    def greet(d, _):
        pl.semaphore_signal(barrier, inc=1, device_id=zx_dev(d)[0], device_id_type=MESH)
        return 0

    lax.fori_loop(1, ROW, greet, 0)
    for d in range(1, NY):
        pl.semaphore_signal(barrier, inc=1, device_id=y_dev(d)[0], device_id_type=MESH)
    pl.semaphore_signal(barrier, inc=1, device_id=sib, device_id_type=MESH)
    pl.semaphore_signal(barrier, inc=1, device_id=pair, device_id_type=MESH)

    loads = [
        pltpu.make_async_copy(w, wv.at[i], w_sem.at[i])
        for i, w in enumerate((gw_hbm, uw_hbm, dw_hbm))
    ]
    for load in loads:
        load.start()
    for a, ref in enumerate((tok_ref, cot_ref)):
        row = ref[...].astype(F32)
        for k in range(width // 128):
            own32[pl.ds(a * (width // 128) + k, 1), :] = row[:, k * 128 : (k + 1) * 128]
    for s in range(2 * parts):
        own[s] = own32[s * ROW : (s + 1) * ROW, :].astype(BF)
        zxb[s, zx] = own[s]
    pl.semaphore_wait(barrier, ROW - 1 + NY - 1 + 2)

    for s in range(2 * parts):

        def send(d, _, s=s):
            pltpu.make_async_remote_copy(
                src_ref=own.at[s], dst_ref=zxb.at[s, zx],
                send_sem=zx_s.at[s], recv_sem=zx_r.at[s],
                device_id=zx_dev(d)[0], device_id_type=MESH,
            ).start()
            return 0

        lax.fori_loop(1, ROW, send, 0)

    def block(ref, s, yy, cc):
        rows = pl.ds(pl.multiple_of(cc * HALF + yy * ROW, ROW), ROW)
        return ref.at[s // parts, rows, pl.ds((s % parts) * wide, wide)]

    def to_y(s, d):
        return pltpu.make_async_remote_copy(
            src_ref=block(whole, s, y, c), dst_ref=block(whole, s, y, c),
            send_sem=y_s.at[s, d - 1], recv_sem=y_r.at[s, d - 1],
            device_id=y_dev(d)[0], device_id_type=MESH,
        )

    def to_sib(s, d):
        yy = lax.rem(y + NY - d, NY)
        return pltpu.make_async_remote_copy(
            src_ref=block(whole, s, yy, c), dst_ref=block(whole, s, yy, c),
            send_sem=sib_s.at[s, d], recv_sem=sib_r.at[s, d],
            device_id=sib, device_id_type=MESH,
        )

    def gather_zx(s):
        some = zxb.at[s, pl.ds(0, ROW - 1)]
        pltpu.make_async_copy(some, some, zx_r.at[s]).wait()
        turned = jnp.swapaxes(zxb[s], 0, 1)
        rows = pl.ds(pl.multiple_of(c * HALF + y * ROW, ROW), ROW)
        for k in range(ROW):
            col = (s % parts) * wide + k * 128
            whole[s // parts, rows, pl.ds(col, 128)] = turned[k]
        for d in (2, 1, 3):
            to_y(s, d).start()
        to_sib(s, 0).start()

    def gather_y(s):
        for d in (1, 3, 2):
            to_y(s, d).wait_recv()
            to_sib(s, d).start()

    def gather_sib(s):
        for d in (0, 1, 3, 2):
            to_sib(s, d).wait_recv()

    def piece(ref, i, s):
        return ref[i, :, pl.ds((s % parts) * wide, wide)]

    def to_pair(i):
        return pltpu.make_async_remote_copy(
            src_ref=wis.at[i], dst_ref=wir.at[i], send_sem=wi_s.at[i], recv_sem=wi_r.at[i],
            device_id=pair, device_id_type=MESH,
        )

    gather_zx(0)
    gather_zx(1)
    gather_y(0)
    gather_zx(2)
    gather_y(1)
    gather_sib(0)
    loads[0].wait()
    loads[1].wait()
    gate = nt(piece(wv, 0, 0), piece(whole, 0, 0))
    up = nt(piece(wv, 1, 0), piece(whole, 0, 0))
    gather_zx(3)
    gather_y(2)
    gather_sib(1)
    gate += nt(piece(wv, 0, 1), piece(whole, 0, 1))
    wis[0] = gate.astype(BF)
    to_pair(0).start()
    up += nt(piece(wv, 1, 1), piece(whole, 0, 1))
    wis[1] = up.astype(BF)
    to_pair(1).start()
    gather_y(3)
    gather_sib(2)
    loads[2].wait()
    dhid = nt(piece(wv, 2, 2), piece(whole, 1, 2))
    gather_sib(3)
    dhid += nt(piece(wv, 2, 3), piece(whole, 1, 3))
    wis[2] = dhid.astype(BF)
    to_pair(2).start()
    saved = [pltpu.make_async_copy(whole, all_out, out_sem.at[0])]
    saved[0].start()

    to_pair(0).wait_recv()
    to_pair(1).wait_recv()
    gate = gate + wir[0].astype(F32)
    up = up + wir[1].astype(F32)
    sig = jax.nn.sigmoid(gate)
    act = gate * sig
    hidden = (act * up).astype(BF)
    acts[0] = hidden
    tp[0] = jnp.transpose(hidden.astype(F32)).astype(BF)

    rows_own = pl.ds(pl.multiple_of(c * HALF, HALF), HALF)
    rows_sib = pl.ds(pl.multiple_of((1 - c) * HALF, HALF), HALF)

    def to_core(a, h):
        return pltpu.make_async_remote_copy(
            src_ref=cs.at[a, h], dst_ref=cr.at[a, h], send_sem=c_s.at[a, h],
            recv_sem=c_r.at[a, h], device_id=sib, device_id_type=MESH,
        )

    def term(a, h):
        cols = pl.ds(h * wide, wide)
        for part, rows in ((0, rows_sib), (1, rows_own)):
            if a == 0:
                value = nn(tp[0, rows, :], wv[2, :, cols])
            else:
                value = nn(tp[1, rows, :], wv[0, :, cols]) + nn(tp[2, rows, :], wv[1, :, cols])
            if part == 0:
                cs[a, h] = value.astype(BF)
                to_core(a, h).start()
            else:
                mine[a, h] = value

    def to_row(a, h, d):
        there = pl.ds(pl.multiple_of(lax.rem(y + d, NY) * ROW, ROW), ROW)
        return pltpu.make_async_remote_copy(
            src_ref=ys.at[a, h, there], dst_ref=yr.at[a, h, d - 1], send_sem=ry_s.at[a, h, d - 1],
            recv_sem=ry_r.at[a, h, d - 1], device_id=y_dev(d)[0], device_id_type=MESH,
        )

    def scatter_core(a, h):
        to_core(a, h).wait_recv()
        value = mine[a, h] + cr[a, h].astype(F32)
        mine[a, h] = value
        ys[a, h] = value.astype(BF)
        for d in (2, 1, 3):
            to_row(a, h, d).start()

    def scatter_y(a, h):
        here = pl.ds(pl.multiple_of(y * ROW, ROW), ROW)
        value = mine[a, h, here]
        for d in (1, 3, 2):
            to_row(a, h, d).wait_recv()
            value = value + yr[a, h, d - 1].astype(F32)
        value = value.astype(BF)
        split = jnp.concatenate(
            [value[:, k * 128 : (k + 1) * 128].reshape(1, ROW, 128) for k in range(ROW)], axis=0
        )
        zs[a, h] = jnp.swapaxes(split, 0, 1)
        zr[a, h, 0] = zs[a, h, zx]

        def send(d, _):
            there, t = zx_dev(d)
            pltpu.make_async_remote_copy(
                src_ref=zs.at[a, h, t], dst_ref=zr.at[a, h, d], send_sem=rz_s.at[a, h],
                recv_sem=rz_r.at[a, h], device_id=there, device_id_type=MESH,
            ).start()
            return 0

        lax.fori_loop(1, ROW, send, 0)

    def scatter_zx(a, h):
        some = zr.at[a, h, pl.ds(1, ROW - 1)]
        pltpu.make_async_copy(some, some, rz_r.at[a, h]).wait()
        rows_out[a, h * ROW : (h + 1) * ROW, :] = jnp.sum(zr[a, h].astype(F32), axis=0)

    term(0, 0)
    term(0, 1)
    to_pair(2).wait_recv()
    dhid = dhid + wir[2].astype(F32)
    dgate = (dhid * up * sig * (1.0 + gate * (1.0 - sig))).astype(BF)
    dup = (dhid * act).astype(BF)
    acts[1] = dgate
    acts[2] = dup
    saved.append(pltpu.make_async_copy(acts, act_out, out_sem.at[1]))
    saved[1].start()
    tp[1] = jnp.transpose(dgate.astype(F32)).astype(BF)
    tp[2] = jnp.transpose(dup.astype(F32)).astype(BF)
    scatter_core(0, 0)
    term(1, 0)
    scatter_core(0, 1)
    term(1, 1)
    scatter_core(1, 0)
    scatter_core(1, 1)
    scatter_y(0, 0)
    scatter_y(0, 1)
    scatter_y(1, 0)
    scatter_y(1, 1)
    for a in range(2):
        for h in range(parts):
            scatter_zx(a, h)

    for s in range(2 * parts):
        some = zxb.at[s, pl.ds(0, ROW - 1)]
        pltpu.make_async_copy(some, some, zx_s.at[s]).wait()
        for d in range(1, NY):
            to_y(s, d).wait_send()
        for d in range(NY):
            to_sib(s, d).wait_send()
    for i in range(3):
        to_pair(i).wait_send()
    for a in range(2):
        for h in range(parts):
            to_core(a, h).wait_send()
            for d in range(1, NY):
                to_row(a, h, d).wait_send()
            some = zs.at[a, h, pl.ds(0, ROW - 1)]
            pltpu.make_async_copy(some, some, rz_s.at[a, h]).wait()
    for copy in saved:
        copy.wait()


def grads_kernel(all_ref, act_ref, rows_ref, out_ref, gin_ref, gg_ref, gu_ref, gd_ref):
    gd_ref[...] = nn(act_ref[0], all_ref[1]).astype(BF)
    gg_ref[...] = nn(act_ref[1], all_ref[0]).astype(BF)
    gu_ref[...] = nn(act_ref[2], all_ref[0]).astype(BF)

    @pl.when(pl.program_id(0) == 0)
    def _():
        for a, ref in enumerate((out_ref, gin_ref)):
            for k in range(rows_ref.shape[1]):
                ref[:, k * 128 : (k + 1) * 128] = rows_ref[a, k : k + 1, :].astype(BF)


def per_device(tokens, gate_weight, up_weight, down_weight, cotangent):
    units, width = gate_weight.shape
    tokens_all = ROW * NY * NC
    wide = ROW * 128
    parts = width // wide
    st = 2 * parts
    vm = pl.BlockSpec(memory_space=pltpu.VMEM)
    hbm = pl.BlockSpec(memory_space=pl.ANY)
    sem = pltpu.SemaphoreType.DMA
    whole, acts, rows = pl.pallas_call(
        exchange_kernel,
        out_shape=[
            jax.ShapeDtypeStruct((2, tokens_all, width), BF),
            jax.ShapeDtypeStruct((3, units, tokens_all), BF),
            jax.ShapeDtypeStruct((2, width // 128, 128), F32),
        ],
        in_specs=[vm, vm, hbm, hbm, hbm],
        out_specs=[hbm, hbm, vm],
        scratch_shapes=[
            pltpu.VMEM((3, units, width), BF),
            pltpu.VMEM((2 * width // 128, 128), F32),
            pltpu.VMEM((st, ROW, 128), BF),
            pltpu.VMEM((st, ROW, ROW, 128), BF),
            pltpu.VMEM((2, tokens_all, width), BF),
            pltpu.VMEM((3, units, tokens_all), BF),
            pltpu.VMEM((3, units, tokens_all), BF),
            pltpu.VMEM((3, tokens_all, units), BF),
            pltpu.VMEM((2, parts, HALF, wide), BF),
            pltpu.VMEM((2, parts, HALF, wide), BF),
            pltpu.VMEM((2, parts, HALF, wide), F32),
            pltpu.VMEM((2, parts, HALF, wide), BF),
            pltpu.VMEM((2, parts, NY - 1, ROW, wide), BF),
            pltpu.VMEM((2, parts, ROW, ROW, 128), BF),
            pltpu.VMEM((2, parts, ROW, ROW, 128), BF),
            pltpu.VMEM((3, units, tokens_all), BF),
            sem((3,)), sem((st,)), sem((st,)), sem((st, NY - 1)), sem((st, NY - 1)),
            sem((st, NY)), sem((st, NY)), sem((3,)), sem((3,)),
            sem((2, parts)), sem((2, parts)), sem((2, parts, NY - 1)), sem((2, parts, NY - 1)),
            sem((2, parts)), sem((2, parts)), sem((2,)),
        ],
        compiler_params=pltpu.CompilerParams(
            collective_id=0, has_side_effects=True, vmem_limit_bytes=48 << 20
        ),
        name="exchange",
    )(tokens, cotangent, gate_weight, up_weight, down_weight)
    step = 512
    big = pl.BlockSpec((units, step), lambda j: (0, j))
    small = pl.BlockSpec((1, width), lambda j: (0, 0))
    output, grad_input, grad_gate, grad_up, grad_down = pl.pallas_call(
        grads_kernel,
        grid=(width // step,),
        out_shape=[jax.ShapeDtypeStruct((1, width), BF)] * 2
        + [jax.ShapeDtypeStruct((units, width), BF)] * 3,
        in_specs=[
            pl.BlockSpec((2, tokens_all, step), lambda j: (0, 0, j)),
            pl.BlockSpec((3, units, tokens_all), lambda j: (0, 0, 0)),
            pl.BlockSpec((2, width // 128, 128), lambda j: (0, 0, 0)),
        ],
        out_specs=[small, small, big, big, big],
        compiler_params=pltpu.CompilerParams(vmem_limit_bytes=48 << 20),
        name="grads",
    )(whole, acts, rows)
    return output, grad_input, grad_gate, grad_up, grad_down


def solution(mesh):
    spec = P(("tok", "wo"), "wi")
    return jax.shard_map(
        per_device, mesh=mesh, in_specs=(spec,) * 5, out_specs=(spec,) * 5, check_vma=False
    )
```

```python
import functools

import jax
import jax.numpy as jnp
from jax import lax
from jax.experimental import pallas as pl
from jax.experimental.pallas import tpu as pltpu
from jax.sharding import PartitionSpec as P

MESH = pl.DeviceIdType.MESH
BF = jnp.bfloat16
F32 = jnp.float32
NY, NZ, NX, NC = 4, 8, 2, 2
ROW = NZ * NX
HALF = NY * ROW
TURN_G = 1
TURN_S = (0, 1)


def nt(left, right):
    return lax.dot_general(left, right, (((1,), (1,)), ((), ())), preferred_element_type=F32)


def nn(left, right):
    return jnp.dot(left, right, preferred_element_type=F32)


def exchange_kernel(
    tok_hbm, cot_hbm, gw_hbm, uw_hbm, dw_hbm,
    out_ref, gin_ref, gg_ref, gu_ref, gd_ref,
    raw, wv, own32, own, zxb, whole, wis, wir, tp, cs, cr, mine, ys, yr, zs, zr,
    w_sem, zx_s, zx_r, y_s, y_r, sib_s, sib_r, wi_s, wi_r,
    c_s, c_r, ry_s, ry_r, rz_s, rz_r,
    gq, sq, rq, uq, vq, q_s, q_r, qs_s, qs_r, qy_s, qy_r,
):
    width = wv.shape[2]
    parts = width // (ROW * 128)
    wide = ROW * 128
    tok_i, wi_i, wo_i = lax.axis_index("tok"), lax.axis_index("wi"), lax.axis_index("wo")
    y, z = tok_i // NZ, lax.rem(tok_i, NZ)
    xh, c = wo_i // NC, lax.rem(wo_i, NC)
    zx = z * NX + xh

    def zx_dev(d):
        t = lax.rem(zx + d, ROW)
        return (y * NZ + t // NX, wi_i, lax.rem(t, NX) * NC + c), t

    def y_dev(d):
        t = lax.rem(y + d, NY)
        return (t * NZ + z, wi_i, wo_i), t

    sib = (tok_i, wi_i, xh * NC + (1 - c))
    pair = (tok_i, 1 - wi_i, wo_i)

    loads = [
        pltpu.make_async_copy(w, there, w_sem.at[i])
        for i, (w, there) in enumerate(
            (
                (gw_hbm, wv.at[0]), (uw_hbm, wv.at[1]), (dw_hbm, wv.at[2]),
                (tok_hbm, raw.at[0]), (cot_hbm, raw.at[1]),
            )
        )
    ]
    for i in (3, 4, 0, 1, 2):
        loads[i].start()

    barrier = pltpu.get_barrier_semaphore()

    def greet(d, _):
        pl.semaphore_signal(barrier, inc=1, device_id=zx_dev(d)[0], device_id_type=MESH)
        return 0

    lax.fori_loop(1, ROW, greet, 0)
    for d in range(1, NY):
        pl.semaphore_signal(barrier, inc=1, device_id=y_dev(d)[0], device_id_type=MESH)
    pl.semaphore_signal(barrier, inc=1, device_id=sib, device_id_type=MESH)
    pl.semaphore_signal(barrier, inc=1, device_id=pair, device_id_type=MESH)

    for a in range(2):
        loads[3 + a].wait()
        row = raw[a].astype(F32)
        for k in range(width // 128):
            own32[pl.ds(a * (width // 128) + k, 1), :] = row[:, k * 128 : (k + 1) * 128]
    for s in range(2 * parts):
        own[s] = own32[s * ROW : (s + 1) * ROW, :].astype(BF)
        zxb[s, zx] = own[s]
    pl.semaphore_wait(barrier, ROW - 1 + NY - 1 + 2)

    straight = [s for s in range(2 * parts) if s != TURN_G]
    gq[zx, y] = own[TURN_G]

    def turn_y(d):
        return pltpu.make_async_remote_copy(
            src_ref=own.at[TURN_G], dst_ref=gq.at[zx, y],
            send_sem=q_s.at[0], recv_sem=q_r.at[0],
            device_id=y_dev(d)[0], device_id_type=MESH,
        )

    for d in (2, 1, 3):
        turn_y(d).start()

    for s in straight:

        def send(d, _, s=s):
            pltpu.make_async_remote_copy(
                src_ref=own.at[s], dst_ref=zxb.at[s, zx],
                send_sem=zx_s.at[s], recv_sem=zx_r.at[s],
                device_id=zx_dev(d)[0], device_id_type=MESH,
            ).start()
            return 0

        lax.fori_loop(1, ROW, send, 0)

    def turn_zx():
        some = gq.at[0, pl.ds(0, NY - 1)]
        pltpu.make_async_copy(some, some, q_r.at[0]).wait()

        def send(d, _):
            pltpu.make_async_remote_copy(
                src_ref=gq.at[zx], dst_ref=gq.at[zx], send_sem=q_s.at[1], recv_sem=q_r.at[1],
                device_id=zx_dev(d)[0], device_id_type=MESH,
            ).start()
            return 0

        lax.fori_loop(1, ROW, send, 0)

    def turn_sib():
        rows = pl.ds(pl.multiple_of(c * HALF, HALF), HALF)
        ref = whole.at[TURN_G // parts, rows, pl.ds((TURN_G % parts) * wide, wide)]
        return pltpu.make_async_remote_copy(
            src_ref=ref, dst_ref=ref, send_sem=q_s.at[2], recv_sem=q_r.at[2],
            device_id=sib, device_id_type=MESH,
        )

    def turn_in():
        some = gq.at[pl.ds(0, ROW - 1)]
        pltpu.make_async_copy(some, some, q_r.at[1]).wait()
        for yy in range(NY):
            turned = jnp.swapaxes(gq[:, yy], 0, 1)
            rows = pl.ds(pl.multiple_of(c * HALF + yy * ROW, ROW), ROW)
            for k in range(ROW):
                col = (TURN_G % parts) * wide + k * 128
                whole[TURN_G // parts, rows, pl.ds(col, 128)] = turned[k]
        turn_sib().start()

    def block(ref, s, yy, cc):
        rows = pl.ds(pl.multiple_of(cc * HALF + yy * ROW, ROW), ROW)
        return ref.at[s // parts, rows, pl.ds((s % parts) * wide, wide)]

    def to_y(s, d):
        return pltpu.make_async_remote_copy(
            src_ref=block(whole, s, y, c), dst_ref=block(whole, s, y, c),
            send_sem=y_s.at[s, d - 1], recv_sem=y_r.at[s, d - 1],
            device_id=y_dev(d)[0], device_id_type=MESH,
        )

    def to_sib(s, d):
        yy = lax.rem(y + NY - d, NY)
        return pltpu.make_async_remote_copy(
            src_ref=block(whole, s, yy, c), dst_ref=block(whole, s, yy, c),
            send_sem=sib_s.at[s, d], recv_sem=sib_r.at[s, d],
            device_id=sib, device_id_type=MESH,
        )

    def gather_zx(s):
        some = zxb.at[s, pl.ds(0, ROW - 1)]
        pltpu.make_async_copy(some, some, zx_r.at[s]).wait()
        turned = jnp.swapaxes(zxb[s], 0, 1)
        rows = pl.ds(pl.multiple_of(c * HALF + y * ROW, ROW), ROW)
        for k in range(ROW):
            col = (s % parts) * wide + k * 128
            whole[s // parts, rows, pl.ds(col, 128)] = turned[k]
        for d in (2, 1, 3):
            to_y(s, d).start()
        to_sib(s, 0).start()

    def gather_y(s):
        for d in (1, 3, 2):
            to_y(s, d).wait_recv()
            to_sib(s, d).start()

    def gather_sib(s):
        for d in (0, 1, 3, 2):
            to_sib(s, d).wait_recv()

    def piece(ref, i, s):
        return ref[i, :, pl.ds((s % parts) * wide, wide)]

    def to_pair(i):
        return pltpu.make_async_remote_copy(
            src_ref=wis.at[i], dst_ref=wir.at[i], send_sem=wi_s.at[i], recv_sem=wi_r.at[i],
            device_id=pair, device_id_type=MESH,
        )

    turn_zx()
    for s in straight:
        gather_zx(s)
    gather_y(0)
    turn_in()
    gather_y(2)
    gather_sib(0)
    loads[0].wait()
    loads[1].wait()
    gate = nt(piece(wv, 0, 0), piece(whole, 0, 0))
    up = nt(piece(wv, 1, 0), piece(whole, 0, 0))
    turn_sib().wait_recv()
    gate += nt(piece(wv, 0, 1), piece(whole, 0, 1))
    wis[0] = gate.astype(BF)
    to_pair(0).start()
    up += nt(piece(wv, 1, 1), piece(whole, 0, 1))
    wis[1] = up.astype(BF)
    to_pair(1).start()
    gather_y(3)
    gather_sib(2)
    loads[2].wait()
    dhid = nt(piece(wv, 2, 2), piece(whole, 1, 2))
    gather_sib(3)
    dhid += nt(piece(wv, 2, 3), piece(whole, 1, 3))
    wis[2] = dhid.astype(BF)
    to_pair(2).start()

    to_pair(0).wait_recv()
    to_pair(1).wait_recv()
    gate = gate + wir[0].astype(F32)
    up = up + wir[1].astype(F32)
    sig = jax.nn.sigmoid(gate)
    act = gate * sig
    hidden = (act * up).astype(BF)
    tp[0] = jnp.transpose(hidden.astype(F32)).astype(BF)

    rows_own = pl.ds(pl.multiple_of(c * HALF, HALF), HALF)
    rows_sib = pl.ds(pl.multiple_of((1 - c) * HALF, HALF), HALF)

    def to_core(a, h):
        return pltpu.make_async_remote_copy(
            src_ref=cs.at[a, h], dst_ref=cr.at[a, h], send_sem=c_s.at[a, h],
            recv_sem=c_r.at[a, h], device_id=sib, device_id_type=MESH,
        )

    def term(a, h, rows):
        cols = pl.ds(h * wide, wide)
        if a == 0:
            return nn(tp[0, rows, :], wv[2, :, cols])
        return nn(tp[1, rows, :], wv[0, :, cols]) + nn(tp[2, rows, :], wv[1, :, cols])

    def terms(a):
        for h in range(parts):
            cs[a, h] = term(a, h, rows_sib).astype(BF)
            to_core(a, h).start()
        for h in range(parts):
            mine[a, h] = term(a, h, rows_own)

    def to_row(a, h, d):
        there = pl.ds(pl.multiple_of(lax.rem(y + d, NY) * ROW, ROW), ROW)
        return pltpu.make_async_remote_copy(
            src_ref=ys.at[a, h, there], dst_ref=yr.at[a, h, d - 1], send_sem=ry_s.at[a, h, d - 1],
            recv_sem=ry_r.at[a, h, d - 1], device_id=y_dev(d)[0], device_id_type=MESH,
        )

    def split(value):
        pieces = [value[:, k * 128 : (k + 1) * 128].reshape(1, ROW, 128) for k in range(ROW)]
        return jnp.swapaxes(jnp.concatenate(pieces, axis=0), 0, 1)

    def turn_out(value):
        for yy in range(NY):
            sq[:, yy] = split(value[yy * ROW : (yy + 1) * ROW])
        rq[0] = sq[zx]

        def send(d, _):
            there, t = zx_dev(d)
            pltpu.make_async_remote_copy(
                src_ref=sq.at[t], dst_ref=rq.at[d], send_sem=qs_s.at[0], recv_sem=qs_r.at[0],
                device_id=there, device_id_type=MESH,
            ).start()
            return 0

        lax.fori_loop(1, ROW, send, 0)

    def turn_back(d):
        return pltpu.make_async_remote_copy(
            src_ref=uq.at[lax.rem(y + d, NY)], dst_ref=vq.at[d], send_sem=qy_s.at[d - 1],
            recv_sem=qy_r.at[d - 1], device_id=y_dev(d)[0], device_id_type=MESH,
        )

    def turn_sum():
        some = rq.at[pl.ds(1, ROW - 1)]
        pltpu.make_async_copy(some, some, qs_r.at[0]).wait()
        uq[...] = jnp.sum(rq[...].astype(F32), axis=0).astype(BF)
        for d in (2, 1, 3):
            turn_back(d).start()
        vq[0] = uq[y]

    def scatter_core(a, h):
        to_core(a, h).wait_recv()
        value = mine[a, h] + cr[a, h].astype(F32)
        if (a, h) == TURN_S:
            turn_out(value.astype(BF))
            return
        mine[a, h] = value
        ys[a, h] = value.astype(BF)
        for d in (2, 1, 3):
            to_row(a, h, d).start()

    def scatter_y(a, h):
        here = pl.ds(pl.multiple_of(y * ROW, ROW), ROW)
        value = mine[a, h, here]
        for d in (1, 3, 2):
            to_row(a, h, d).wait_recv()
            value = value + yr[a, h, d - 1].astype(F32)
        value = value.astype(BF)
        zs[a, h] = split(value)
        zr[a, h, 0] = zs[a, h, zx]

        def send(d, _):
            there, t = zx_dev(d)
            pltpu.make_async_remote_copy(
                src_ref=zs.at[a, h, t], dst_ref=zr.at[a, h, d], send_sem=rz_s.at[a, h],
                recv_sem=rz_r.at[a, h], device_id=there, device_id_type=MESH,
            ).start()
            return 0

        lax.fori_loop(1, ROW, send, 0)

    def scatter_zx(a, h):
        if (a, h) == TURN_S:
            for d in (1, 3, 2):
                turn_back(d).wait_recv()
            total = jnp.sum(vq[...].astype(F32), axis=0).astype(BF)
        else:
            some = zr.at[a, h, pl.ds(1, ROW - 1)]
            pltpu.make_async_copy(some, some, rz_r.at[a, h]).wait()
            total = jnp.sum(zr[a, h].astype(F32), axis=0).astype(BF)
        for k in range(ROW):
            col = h * wide + k * 128
            (out_ref, gin_ref)[a][:, col : col + 128] = total[k : k + 1, :]

    def grad(ref, act_value, a):
        for j in range(width // 1024):
            cols = pl.ds(j * 1024, 1024)
            ref[:, cols] = nn(act_value, whole[a, :, cols]).astype(BF)

    terms(0)
    scatter_core(0, 0)
    scatter_core(0, 1)
    to_pair(2).wait_recv()
    dhid = dhid + wir[2].astype(F32)
    dgate = (dhid * up * sig * (1.0 + gate * (1.0 - sig))).astype(BF)
    dup = (dhid * act).astype(BF)
    tp[1] = jnp.transpose(dgate.astype(F32)).astype(BF)
    tp[2] = jnp.transpose(dup.astype(F32)).astype(BF)
    terms(1)
    for h in range(parts):
        scatter_core(1, h)
    scatter_y(0, 0)
    turn_sum()
    scatter_y(1, 0)
    scatter_y(1, 1)
    grad(gd_ref, hidden, 1)
    grad(gg_ref, dgate, 0)
    grad(gu_ref, dup, 0)
    for a in range(2):
        for h in range(parts):
            scatter_zx(a, h)

    for s in straight:
        some = zxb.at[s, pl.ds(0, ROW - 1)]
        pltpu.make_async_copy(some, some, zx_s.at[s]).wait()
        for d in range(1, NY):
            to_y(s, d).wait_send()
        for d in range(NY):
            to_sib(s, d).wait_send()
    some = gq.at[0, pl.ds(0, NY - 1)]
    pltpu.make_async_copy(some, some, q_s.at[0]).wait()
    some = gq.at[pl.ds(0, ROW - 1)]
    pltpu.make_async_copy(some, some, q_s.at[1]).wait()
    turn_sib().wait_send()
    for i in range(3):
        to_pair(i).wait_send()
    for a in range(2):
        for h in range(parts):
            to_core(a, h).wait_send()
            if (a, h) == TURN_S:
                some = sq.at[pl.ds(0, ROW - 1)]
                pltpu.make_async_copy(some, some, qs_s.at[0]).wait()
                for d in range(1, NY):
                    turn_back(d).wait_send()
                continue
            for d in range(1, NY):
                to_row(a, h, d).wait_send()
            some = zs.at[a, h, pl.ds(0, ROW - 1)]
            pltpu.make_async_copy(some, some, rz_s.at[a, h]).wait()


def store_kernel(*refs):
    sems = refs[-1]
    n = (len(refs) - 1) // 2
    copies = [pltpu.make_async_copy(refs[i], refs[n + i], sems.at[i]) for i in range(n)]
    for copy in copies:
        copy.start()
    for copy in copies:
        copy.wait()


def per_device(tokens, gate_weight, up_weight, down_weight, cotangent):
    units, width = gate_weight.shape
    tokens_all = ROW * NY * NC
    wide = ROW * 128
    parts = width // wide
    st = 2 * parts
    vm = pl.BlockSpec(memory_space=pltpu.VMEM)
    hbm = pl.BlockSpec(memory_space=pltpu.HBM)
    sem = pltpu.SemaphoreType.DMA
    shapes = [jax.ShapeDtypeStruct((1, width), BF)] * 2
    shapes += [jax.ShapeDtypeStruct((units, width), BF)] * 3
    results = pl.pallas_call(
        exchange_kernel,
        out_shape=shapes,
        in_specs=[hbm] * 5,
        out_specs=[vm] * 5,
        scratch_shapes=[
            pltpu.VMEM((2, 1, width), BF),
            pltpu.VMEM((3, units, width), BF),
            pltpu.VMEM((2 * width // 128, 128), F32),
            pltpu.VMEM((st, ROW, 128), BF),
            pltpu.VMEM((st, ROW, ROW, 128), BF),
            pltpu.VMEM((2, tokens_all, width), BF),
            pltpu.VMEM((3, units, tokens_all), BF),
            pltpu.VMEM((3, units, tokens_all), BF),
            pltpu.VMEM((3, tokens_all, units), BF),
            pltpu.VMEM((2, parts, HALF, wide), BF),
            pltpu.VMEM((2, parts, HALF, wide), BF),
            pltpu.VMEM((2, parts, HALF, wide), F32),
            pltpu.VMEM((2, parts, HALF, wide), BF),
            pltpu.VMEM((2, parts, NY - 1, ROW, wide), BF),
            pltpu.VMEM((2, parts, ROW, ROW, 128), BF),
            pltpu.VMEM((2, parts, ROW, ROW, 128), BF),
            sem((5,)), sem((st,)), sem((st,)), sem((st, NY - 1)), sem((st, NY - 1)),
            sem((st, NY)), sem((st, NY)), sem((3,)), sem((3,)),
            sem((2, parts)), sem((2, parts)), sem((2, parts, NY - 1)), sem((2, parts, NY - 1)),
            sem((2, parts)), sem((2, parts)),
            pltpu.VMEM((ROW, NY, ROW, 128), BF),
            pltpu.VMEM((ROW, NY, ROW, 128), BF),
            pltpu.VMEM((ROW, NY, ROW, 128), BF),
            pltpu.VMEM((NY, ROW, 128), BF),
            pltpu.VMEM((NY, ROW, 128), BF),
            sem((3,)), sem((3,)), sem((1,)), sem((1,)), sem((NY - 1,)), sem((NY - 1,)),
        ],
        compiler_params=pltpu.CompilerParams(
            collective_id=0, has_side_effects=True, vmem_limit_bytes=48 << 20
        ),
        name="exchange",
    )(tokens, cotangent, gate_weight, up_weight, down_weight)
    return tuple(
        pl.pallas_call(
            store_kernel,
            out_shape=shapes,
            in_specs=[vm] * 5,
            out_specs=[hbm] * 5,
            scratch_shapes=[sem((5,))],
            compiler_params=pltpu.CompilerParams(vmem_limit_bytes=1 << 20),
            name="store",
        )(*results)
    )


def solution(mesh):
    spec = P(("tok", "wo"), "wi")
    return jax.shard_map(
        per_device, mesh=mesh, in_specs=(spec,) * 5, out_specs=(spec,) * 5, check_vma=False
    )
```

```python
import functools

import jax
import jax.numpy as jnp
from jax import lax
from jax.experimental import pallas as pl
from jax.experimental.pallas import tpu as pltpu
from jax.sharding import PartitionSpec as P

MESH = pl.DeviceIdType.MESH
BF = jnp.bfloat16
F32 = jnp.float32
NY, NZ, NX, NC = 4, 8, 2, 2
ROW = NZ * NX
HALF = NY * ROW
TURN_G = 1
TURN_S = (0, 1)


def nt(left, right):
    return lax.dot_general(left, right, (((1,), (1,)), ((), ())), preferred_element_type=F32)


def nn(left, right):
    return jnp.dot(left, right, preferred_element_type=F32)


def exchange_kernel(
    tok_hbm, cot_hbm, gw_hbm, uw_hbm, dw_hbm,
    out_ref, gin_ref, gg_ref, gu_ref, gd_ref,
    raw, wv, own32, own, zxb, whole, wis, wir, acts, gact, mine, ys, yr, zs, zr,
    w_sem, zx_s, zx_r, y_s, y_r, sw_s, sw_r, st_s, st_r, sa_s, sa_r, wi_s, wi_r,
    ry_s, ry_r, rz_s, rz_r,
    gq, sq, rq, uq, vq, q_s, q_r, qs_s, qs_r, qy_s, qy_r,
):
    width = wv.shape[3]
    parts = width // (ROW * 128)
    wide = ROW * 128
    tok_i, wi_i, wo_i = lax.axis_index("tok"), lax.axis_index("wi"), lax.axis_index("wo")
    y, z = tok_i // NZ, lax.rem(tok_i, NZ)
    xh, c = wo_i // NC, lax.rem(wo_i, NC)
    zx = z * NX + xh

    def zx_dev(d):
        t = lax.rem(zx + d, ROW)
        return (y * NZ + t // NX, wi_i, lax.rem(t, NX) * NC + c), t

    def y_dev(d):
        t = lax.rem(y + d, NY)
        return (t * NZ + z, wi_i, wo_i), t

    sib = (tok_i, wi_i, xh * NC + (1 - c))
    pair = (tok_i, 1 - wi_i, wo_i)

    loads = [
        pltpu.make_async_copy(w, there, w_sem.at[i])
        for i, (w, there) in enumerate(
            (
                (gw_hbm, wv.at[0, c]), (uw_hbm, wv.at[1, c]), (dw_hbm, wv.at[2, c]),
                (tok_hbm, raw.at[0]), (cot_hbm, raw.at[1]),
            )
        )
    ]
    for i in (3, 4, 0, 1, 2):
        loads[i].start()

    barrier = pltpu.get_barrier_semaphore()

    def greet(d, _):
        pl.semaphore_signal(barrier, inc=1, device_id=zx_dev(d)[0], device_id_type=MESH)
        return 0

    lax.fori_loop(1, ROW, greet, 0)
    for d in range(1, NY):
        pl.semaphore_signal(barrier, inc=1, device_id=y_dev(d)[0], device_id_type=MESH)
    pl.semaphore_signal(barrier, inc=1, device_id=sib, device_id_type=MESH)
    pl.semaphore_signal(barrier, inc=1, device_id=pair, device_id_type=MESH)

    for a in range(2):
        loads[3 + a].wait()
        row = raw[a].astype(F32)
        for k in range(width // 128):
            own32[pl.ds(a * (width // 128) + k, 1), :] = row[:, k * 128 : (k + 1) * 128]
    for s in range(2 * parts):
        own[s] = own32[s * ROW : (s + 1) * ROW, :].astype(BF)
        zxb[s, zx] = own[s]
    pl.semaphore_wait(barrier, ROW - 1 + NY - 1 + 2)

    straight = [s for s in range(2 * parts) if s != TURN_G]
    gq[zx, y] = own[TURN_G]

    def turn_y(d):
        return pltpu.make_async_remote_copy(
            src_ref=own.at[TURN_G], dst_ref=gq.at[zx, y],
            send_sem=q_s.at[0], recv_sem=q_r.at[0],
            device_id=y_dev(d)[0], device_id_type=MESH,
        )

    for d in (2, 1, 3):
        turn_y(d).start()

    for s in straight:

        def send(d, _, s=s):
            pltpu.make_async_remote_copy(
                src_ref=own.at[s], dst_ref=zxb.at[s, zx],
                send_sem=zx_s.at[s], recv_sem=zx_r.at[s],
                device_id=zx_dev(d)[0], device_id_type=MESH,
            ).start()
            return 0

        lax.fori_loop(1, ROW, send, 0)

    def turn_zx():
        some = gq.at[0, pl.ds(0, NY - 1)]
        pltpu.make_async_copy(some, some, q_r.at[0]).wait()

        def send(d, _):
            pltpu.make_async_remote_copy(
                src_ref=gq.at[zx], dst_ref=gq.at[zx], send_sem=q_s.at[1], recv_sem=q_r.at[1],
                device_id=zx_dev(d)[0], device_id_type=MESH,
            ).start()
            return 0

        lax.fori_loop(1, ROW, send, 0)

    def turn_in():
        some = gq.at[pl.ds(0, ROW - 1)]
        pltpu.make_async_copy(some, some, q_r.at[1]).wait()
        for yy in range(NY):
            turned = jnp.swapaxes(gq[:, yy], 0, 1)
            rows = pl.ds(pl.multiple_of(c * HALF + yy * ROW, ROW), ROW)
            for k in range(ROW):
                col = (TURN_G % parts) * wide + k * 128
                whole[TURN_G // parts, rows, pl.ds(col, 128)] = turned[k]

    def block(ref, s, yy, cc):
        rows = pl.ds(pl.multiple_of(cc * HALF + yy * ROW, ROW), ROW)
        return ref.at[s // parts, rows, pl.ds((s % parts) * wide, wide)]

    def to_y(s, d):
        return pltpu.make_async_remote_copy(
            src_ref=block(whole, s, y, c), dst_ref=block(whole, s, y, c),
            send_sem=y_s.at[s, d - 1], recv_sem=y_r.at[s, d - 1],
            device_id=y_dev(d)[0], device_id_type=MESH,
        )

    rows_own = pl.ds(pl.multiple_of(c * HALF, HALF), HALF)

    def to_sib(ref, send_sem, recv_sem, there=None):
        return pltpu.make_async_remote_copy(
            src_ref=ref, dst_ref=ref if there is None else there, send_sem=send_sem,
            recv_sem=recv_sem, device_id=sib, device_id_type=MESH,
        )

    def weights(i):
        return to_sib(wv.at[i, c], sw_s.at[i], sw_r.at[i])

    def share(a):
        return to_sib(whole.at[a, rows_own], st_s.at[a], st_r.at[a])

    def share_act(i):
        return to_sib(acts.at[i, 1 - c], sa_s.at[i], sa_r.at[i], gact.at[i, c])

    def gather_zx(s):
        some = zxb.at[s, pl.ds(0, ROW - 1)]
        pltpu.make_async_copy(some, some, zx_r.at[s]).wait()
        turned = jnp.swapaxes(zxb[s], 0, 1)
        rows = pl.ds(pl.multiple_of(c * HALF + y * ROW, ROW), ROW)
        for k in range(ROW):
            col = (s % parts) * wide + k * 128
            whole[s // parts, rows, pl.ds(col, 128)] = turned[k]
        for d in (2, 1, 3):
            to_y(s, d).start()

    def gather_y(s):
        for d in (1, 3, 2):
            to_y(s, d).wait_recv()

    def dots(i, s):
        cols = pl.ds((s % parts) * wide, wide)
        value = whole[s // parts, rows_own, cols]
        return [nt(value, wv[i, b, :, cols]) for b in range(NC)]

    def add(left, right):
        return [x + y for x, y in zip(left, right)]

    def give_pair(i, values):
        for b in range(NC):
            wis[i, b] = values[b].astype(BF)
        to_pair(i).start()

    def take_pair(i, values):
        to_pair(i).wait_recv()
        return [values[b] + wir[i, b].astype(F32) for b in range(NC)]

    def keep(i, b, value):
        acts[i, b] = value.astype(BF)

    def to_pair(i):
        return pltpu.make_async_remote_copy(
            src_ref=wis.at[i], dst_ref=wir.at[i], send_sem=wi_s.at[i], recv_sem=wi_r.at[i],
            device_id=pair, device_id_type=MESH,
        )

    turn_zx()
    for i in range(3):
        loads[i].wait()
        weights(i).start()
    for s in straight:
        gather_zx(s)
    gather_y(0)
    weights(0).wait_recv()
    gate = dots(0, 0)
    weights(1).wait_recv()
    up = dots(1, 0)
    turn_in()
    gate = add(gate, dots(0, 1))
    give_pair(0, gate)
    up = add(up, dots(1, 1))
    give_pair(1, up)
    share(0).start()
    gather_y(2)
    weights(2).wait_recv()
    dhid = dots(2, 2)
    gather_y(3)
    dhid = add(dhid, dots(2, 3))
    give_pair(2, dhid)
    share(1).start()

    gate = take_pair(0, gate)
    up = take_pair(1, up)
    sig = [jax.nn.sigmoid(v) for v in gate]
    act = [gate[b] * sig[b] for b in range(NC)]
    for b in range(NC):
        keep(0, b, act[b] * up[b])

    def term(a, h):
        cols = pl.ds(h * wide, wide)
        total = None
        for i, w in ((0, 2),) if a == 0 else ((1, 0), (2, 1)):
            for b in range(NC):
                value = nn(acts[i, b], wv[w, b, :, cols])
                total = value if total is None else total + value
        return total

    def to_row(a, h, d):
        there = pl.ds(pl.multiple_of(lax.rem(y + d, NY) * ROW, ROW), ROW)
        return pltpu.make_async_remote_copy(
            src_ref=ys.at[a, h, there], dst_ref=yr.at[a, h, d - 1], send_sem=ry_s.at[a, h, d - 1],
            recv_sem=ry_r.at[a, h, d - 1], device_id=y_dev(d)[0], device_id_type=MESH,
        )

    def split(value):
        pieces = [value[:, k * 128 : (k + 1) * 128].reshape(1, ROW, 128) for k in range(ROW)]
        return jnp.swapaxes(jnp.concatenate(pieces, axis=0), 0, 1)

    def turn_out(value):
        for yy in range(NY):
            sq[:, yy] = split(value[yy * ROW : (yy + 1) * ROW])
        rq[0] = sq[zx]

        def send(d, _):
            there, t = zx_dev(d)
            pltpu.make_async_remote_copy(
                src_ref=sq.at[t], dst_ref=rq.at[d], send_sem=qs_s.at[0], recv_sem=qs_r.at[0],
                device_id=there, device_id_type=MESH,
            ).start()
            return 0

        lax.fori_loop(1, ROW, send, 0)

    def turn_back(d):
        return pltpu.make_async_remote_copy(
            src_ref=uq.at[lax.rem(y + d, NY)], dst_ref=vq.at[d], send_sem=qy_s.at[d - 1],
            recv_sem=qy_r.at[d - 1], device_id=y_dev(d)[0], device_id_type=MESH,
        )

    def turn_sum():
        some = rq.at[pl.ds(1, ROW - 1)]
        pltpu.make_async_copy(some, some, qs_r.at[0]).wait()
        uq[...] = jnp.sum(rq[...].astype(F32), axis=0).astype(BF)
        for d in (2, 1, 3):
            turn_back(d).start()
        vq[0] = uq[y]

    def scatter_first(a, h):
        value = term(a, h)
        if (a, h) == TURN_S:
            turn_out(value.astype(BF))
            return
        mine[a, h] = value
        ys[a, h] = value.astype(BF)
        for d in (2, 1, 3):
            to_row(a, h, d).start()

    def scatter_y(a, h):
        here = pl.ds(pl.multiple_of(y * ROW, ROW), ROW)
        value = mine[a, h, here]
        for d in (1, 3, 2):
            to_row(a, h, d).wait_recv()
            value = value + yr[a, h, d - 1].astype(F32)
        value = value.astype(BF)
        zs[a, h] = split(value)
        zr[a, h, 0] = zs[a, h, zx]

        def send(d, _):
            there, t = zx_dev(d)
            pltpu.make_async_remote_copy(
                src_ref=zs.at[a, h, t], dst_ref=zr.at[a, h, d], send_sem=rz_s.at[a, h],
                recv_sem=rz_r.at[a, h], device_id=there, device_id_type=MESH,
            ).start()
            return 0

        lax.fori_loop(1, ROW, send, 0)

    def scatter_zx(a, h):
        if (a, h) == TURN_S:
            for d in (1, 3, 2):
                turn_back(d).wait_recv()
            total = jnp.sum(vq[...].astype(F32), axis=0).astype(BF)
        else:
            some = zr.at[a, h, pl.ds(1, ROW - 1)]
            pltpu.make_async_copy(some, some, rz_r.at[a, h]).wait()
            total = jnp.sum(zr[a, h].astype(F32), axis=0).astype(BF)
        for k in range(ROW):
            col = h * wide + k * 128
            (out_ref, gin_ref)[a][:, col : col + 128] = total[k : k + 1, :]

    def grad(ref, i, a):
        share_act(i).wait_recv()
        gact[i, c] = acts[i, c]
        both = jnp.concatenate([gact[i, b] for b in range(NC)], axis=0)
        act_value = jnp.transpose(both.astype(F32)).astype(BF)
        for j in range(width // 1024):
            cols = pl.ds(j * 1024, 1024)
            ref[:, cols] = nn(act_value, whole[a, :, cols]).astype(BF)

    scatter_first(0, 0)
    scatter_first(0, 1)
    share_act(0).start()
    dhid = take_pair(2, dhid)
    for b in range(NC):
        keep(1, b, dhid[b] * up[b] * sig[b] * (1.0 + gate[b] * (1.0 - sig[b])))
        keep(2, b, dhid[b] * act[b])
    scatter_first(1, 0)
    scatter_first(1, 1)
    share_act(1).start()
    share_act(2).start()
    scatter_y(0, 0)
    turn_sum()
    scatter_y(1, 0)
    scatter_y(1, 1)
    for a in range(2):
        share(a).wait_recv()
    grad(gd_ref, 0, 1)
    grad(gg_ref, 1, 0)
    grad(gu_ref, 2, 0)
    for a in range(2):
        for h in range(parts):
            scatter_zx(a, h)

    for s in straight:
        some = zxb.at[s, pl.ds(0, ROW - 1)]
        pltpu.make_async_copy(some, some, zx_s.at[s]).wait()
        for d in range(1, NY):
            to_y(s, d).wait_send()
    some = gq.at[0, pl.ds(0, NY - 1)]
    pltpu.make_async_copy(some, some, q_s.at[0]).wait()
    some = gq.at[pl.ds(0, ROW - 1)]
    pltpu.make_async_copy(some, some, q_s.at[1]).wait()
    for i in range(3):
        to_pair(i).wait_send()
        weights(i).wait_send()
        share_act(i).wait_send()
    for a in range(2):
        share(a).wait_send()
    for a in range(2):
        for h in range(parts):
            if (a, h) == TURN_S:
                some = sq.at[pl.ds(0, ROW - 1)]
                pltpu.make_async_copy(some, some, qs_s.at[0]).wait()
                for d in range(1, NY):
                    turn_back(d).wait_send()
                continue
            for d in range(1, NY):
                to_row(a, h, d).wait_send()
            some = zs.at[a, h, pl.ds(0, ROW - 1)]
            pltpu.make_async_copy(some, some, rz_s.at[a, h]).wait()


def store_kernel(*refs):
    sems = refs[-1]
    n = (len(refs) - 1) // 2
    copies = [pltpu.make_async_copy(refs[i], refs[n + i], sems.at[i]) for i in range(n)]
    for copy in copies:
        copy.start()
    for copy in copies:
        copy.wait()


def per_device(tokens, gate_weight, up_weight, down_weight, cotangent):
    units, width = gate_weight.shape
    tokens_all = ROW * NY * NC
    wide = ROW * 128
    parts = width // wide
    st = 2 * parts
    vm = pl.BlockSpec(memory_space=pltpu.VMEM)
    hbm = pl.BlockSpec(memory_space=pltpu.HBM)
    sem = pltpu.SemaphoreType.DMA
    shapes = [jax.ShapeDtypeStruct((1, width), BF)] * 2
    shapes += [jax.ShapeDtypeStruct((units, width), BF)] * 3
    inputs = (tokens, cotangent, gate_weight, up_weight, down_weight)
    results = pl.pallas_call(
        exchange_kernel,
        out_shape=shapes,
        in_specs=[hbm] * 5,
        out_specs=[vm] * 5,
        scratch_shapes=[
            pltpu.VMEM((2, 1, width), BF),
            pltpu.VMEM((3, NC, units, width), BF),
            pltpu.VMEM((2 * width // 128, 128), F32),
            pltpu.VMEM((st, ROW, 128), BF),
            pltpu.VMEM((st, ROW, ROW, 128), BF),
            pltpu.VMEM((2, tokens_all, width), BF),
            pltpu.VMEM((3, NC, HALF, units), BF),
            pltpu.VMEM((3, NC, HALF, units), BF),
            pltpu.VMEM((3, NC, HALF, units), BF),
            pltpu.VMEM((3, NC, HALF, units), BF),
            pltpu.VMEM((2, parts, HALF, wide), F32),
            pltpu.VMEM((2, parts, HALF, wide), BF),
            pltpu.VMEM((2, parts, NY - 1, ROW, wide), BF),
            pltpu.VMEM((2, parts, ROW, ROW, 128), BF),
            pltpu.VMEM((2, parts, ROW, ROW, 128), BF),
            sem((5,)), sem((st,)), sem((st,)), sem((st, NY - 1)), sem((st, NY - 1)),
            sem((3,)), sem((3,)), sem((2,)), sem((2,)), sem((3,)), sem((3,)), sem((3,)), sem((3,)),
            sem((2, parts, NY - 1)), sem((2, parts, NY - 1)),
            sem((2, parts)), sem((2, parts)),
            pltpu.VMEM((ROW, NY, ROW, 128), BF),
            pltpu.VMEM((ROW, NY, ROW, 128), BF),
            pltpu.VMEM((ROW, NY, ROW, 128), BF),
            pltpu.VMEM((NY, ROW, 128), BF),
            pltpu.VMEM((NY, ROW, 128), BF),
            sem((2,)), sem((2,)), sem((1,)), sem((1,)), sem((NY - 1,)), sem((NY - 1,)),
        ],
        compiler_params=pltpu.CompilerParams(
            collective_id=0, has_side_effects=True, vmem_limit_bytes=48 << 20
        ),
        name="exchange",
    )(*[pltpu.with_memory_space_constraint(x, pltpu.HBM) for x in inputs])
    return tuple(
        pl.pallas_call(
            store_kernel,
            out_shape=shapes,
            in_specs=[vm] * 5,
            out_specs=[hbm] * 5,
            scratch_shapes=[sem((5,))],
            compiler_params=pltpu.CompilerParams(vmem_limit_bytes=1 << 20),
            name="store",
        )(*results)
    )


def solution(mesh):
    spec = P(("tok", "wo"), "wi")
    return jax.shard_map(
        per_device, mesh=mesh, in_specs=(spec,) * 5, out_specs=(spec,) * 5, check_vma=False
    )
```

```python
import functools

import jax
import jax.numpy as jnp
from jax import lax
from jax.experimental import pallas as pl
from jax.experimental.pallas import tpu as pltpu
from jax.sharding import PartitionSpec as P

MESH = pl.DeviceIdType.MESH
BF = jnp.bfloat16
F32 = jnp.float32
NY, NZ, NX, NC = 4, 8, 2, 2
ROW = NZ * NX
HALF = NY * ROW
TURN_G = 1
TURN_S = (1, 0)


def nt(left, right):
    return lax.dot_general(left, right, (((1,), (1,)), ((), ())), preferred_element_type=F32)


def nn(left, right):
    return jnp.dot(left, right, preferred_element_type=F32)


def exchange_kernel(
    tok_hbm, cot_hbm, gw_hbm, uw_hbm, dw_hbm,
    out_ref, gin_ref, gg_ref, gu_ref, gd_ref,
    raw, wv, own32, own, zxb, whole, wis, wir, acts, gact, mine, ys, yr, zs, zr,
    w_sem, zx_s, zx_r, y_s, y_r, sw_s, sw_r, st_s, st_r, sa_s, sa_r, wi_s, wi_r,
    ry_s, ry_r, rz_s, rz_r,
    gq, sq, rq, uq, vq, q_s, q_r, qs_s, qs_r, qy_s, qy_r,
):
    width = wv.shape[3]
    parts = width // (ROW * 128)
    wide = ROW * 128
    tok_i, wi_i, wo_i = lax.axis_index("tok"), lax.axis_index("wi"), lax.axis_index("wo")
    y, z = tok_i // NZ, lax.rem(tok_i, NZ)
    xh, c = wo_i // NC, lax.rem(wo_i, NC)
    zx = z * NX + xh

    def zx_dev(d):
        t = lax.rem(zx + d, ROW)
        return (y * NZ + t // NX, wi_i, lax.rem(t, NX) * NC + c), t

    def y_dev(d):
        t = lax.rem(y + d, NY)
        return (t * NZ + z, wi_i, wo_i), t

    sib = (tok_i, wi_i, xh * NC + (1 - c))
    pair = (tok_i, 1 - wi_i, wo_i)

    loads = [
        pltpu.make_async_copy(w, there, w_sem.at[i])
        for i, (w, there) in enumerate(
            (
                (gw_hbm, wv.at[0, c]), (uw_hbm, wv.at[1, c]), (dw_hbm, wv.at[2, c]),
                (tok_hbm, raw.at[0]), (cot_hbm, raw.at[1]),
            )
        )
    ]
    for i in (3, 4, 0, 1, 2):
        loads[i].start()

    barrier = pltpu.get_barrier_semaphore()

    def greet(d, _):
        pl.semaphore_signal(barrier, inc=1, device_id=zx_dev(d)[0], device_id_type=MESH)
        return 0

    lax.fori_loop(1, ROW, greet, 0)
    for d in range(1, NY):
        pl.semaphore_signal(barrier, inc=1, device_id=y_dev(d)[0], device_id_type=MESH)
    pl.semaphore_signal(barrier, inc=1, device_id=sib, device_id_type=MESH)
    pl.semaphore_signal(barrier, inc=1, device_id=pair, device_id_type=MESH)

    for a in range(2):
        loads[3 + a].wait()
        row = raw[a].astype(F32)
        for k in range(width // 128):
            own32[pl.ds(a * (width // 128) + k, 1), :] = row[:, k * 128 : (k + 1) * 128]
    for s in range(2 * parts):
        own[s] = own32[s * ROW : (s + 1) * ROW, :].astype(BF)
        zxb[s, zx] = own[s]
    pl.semaphore_wait(barrier, ROW - 1 + NY - 1 + 2)

    straight = [s for s in range(2 * parts) if s != TURN_G]
    gq[zx, y] = own[TURN_G]

    def turn_y(d):
        return pltpu.make_async_remote_copy(
            src_ref=own.at[TURN_G], dst_ref=gq.at[zx, y],
            send_sem=q_s.at[0], recv_sem=q_r.at[0],
            device_id=y_dev(d)[0], device_id_type=MESH,
        )

    for d in (2, 1, 3):
        turn_y(d).start()

    for s in straight:

        def send(d, _, s=s):
            pltpu.make_async_remote_copy(
                src_ref=own.at[s], dst_ref=zxb.at[s, zx],
                send_sem=zx_s.at[s], recv_sem=zx_r.at[s],
                device_id=zx_dev(d)[0], device_id_type=MESH,
            ).start()
            return 0

        lax.fori_loop(1, ROW, send, 0)

    def turn_zx():
        some = gq.at[0, pl.ds(0, NY - 1)]
        pltpu.make_async_copy(some, some, q_r.at[0]).wait()

        def send(d, _):
            pltpu.make_async_remote_copy(
                src_ref=gq.at[zx], dst_ref=gq.at[zx], send_sem=q_s.at[1], recv_sem=q_r.at[1],
                device_id=zx_dev(d)[0], device_id_type=MESH,
            ).start()
            return 0

        lax.fori_loop(1, ROW, send, 0)

    def turn_in():
        some = gq.at[pl.ds(0, ROW - 1)]
        pltpu.make_async_copy(some, some, q_r.at[1]).wait()
        for yy in range(NY):
            turned = jnp.swapaxes(gq[:, yy], 0, 1)
            rows = pl.ds(pl.multiple_of(c * HALF + yy * ROW, ROW), ROW)
            for k in range(ROW):
                col = (TURN_G % parts) * wide + k * 128
                whole[TURN_G // parts, rows, pl.ds(col, 128)] = turned[k]

    def block(ref, s, yy, cc):
        rows = pl.ds(pl.multiple_of(cc * HALF + yy * ROW, ROW), ROW)
        return ref.at[s // parts, rows, pl.ds((s % parts) * wide, wide)]

    def to_y(s, d):
        return pltpu.make_async_remote_copy(
            src_ref=block(whole, s, y, c), dst_ref=block(whole, s, y, c),
            send_sem=y_s.at[s, d - 1], recv_sem=y_r.at[s, d - 1],
            device_id=y_dev(d)[0], device_id_type=MESH,
        )

    rows_own = pl.ds(pl.multiple_of(c * HALF, HALF), HALF)

    def to_sib(ref, send_sem, recv_sem, there=None):
        return pltpu.make_async_remote_copy(
            src_ref=ref, dst_ref=ref if there is None else there, send_sem=send_sem,
            recv_sem=recv_sem, device_id=sib, device_id_type=MESH,
        )

    def weights(i):
        return to_sib(wv.at[i, c], sw_s.at[i], sw_r.at[i])

    def share(a):
        return to_sib(whole.at[a, rows_own], st_s.at[a], st_r.at[a])

    def share_act(i):
        return to_sib(acts.at[i, 1 - c], sa_s.at[i], sa_r.at[i], gact.at[i, c])

    def gather_zx(s):
        some = zxb.at[s, pl.ds(0, ROW - 1)]
        pltpu.make_async_copy(some, some, zx_r.at[s]).wait()
        turned = jnp.swapaxes(zxb[s], 0, 1)
        rows = pl.ds(pl.multiple_of(c * HALF + y * ROW, ROW), ROW)
        for k in range(ROW):
            col = (s % parts) * wide + k * 128
            whole[s // parts, rows, pl.ds(col, 128)] = turned[k]
        for d in (2, 1, 3):
            to_y(s, d).start()

    def gather_y(s):
        for d in (1, 3, 2):
            to_y(s, d).wait_recv()

    def dots(i, s):
        cols = pl.ds((s % parts) * wide, wide)
        value = whole[s // parts, rows_own, cols]
        return [nt(value, wv[i, b, :, cols]) for b in range(NC)]

    def add(left, right):
        return [x + y for x, y in zip(left, right)]

    def give_pair(i, values):
        for b in range(NC):
            wis[i, b] = values[b].astype(BF)
        to_pair(i).start()

    def take_pair(i, values):
        to_pair(i).wait_recv()
        return [values[b] + wir[i, b].astype(F32) for b in range(NC)]

    def keep(i, b, value):
        acts[i, b] = value.astype(BF)

    def to_pair(i):
        return pltpu.make_async_remote_copy(
            src_ref=wis.at[i], dst_ref=wir.at[i], send_sem=wi_s.at[i], recv_sem=wi_r.at[i],
            device_id=pair, device_id_type=MESH,
        )

    turn_zx()
    for i in range(3):
        loads[i].wait()
        weights(i).start()
    for s in straight:
        gather_zx(s)
    gather_y(0)
    weights(0).wait_recv()
    gate = dots(0, 0)
    weights(1).wait_recv()
    up = dots(1, 0)
    turn_in()
    gate = add(gate, dots(0, 1))
    give_pair(0, gate)
    up = add(up, dots(1, 1))
    give_pair(1, up)
    share(0).start()
    gather_y(2)
    weights(2).wait_recv()
    dhid = dots(2, 2)
    gather_y(3)
    dhid = add(dhid, dots(2, 3))
    give_pair(2, dhid)
    share(1).start()

    gate = take_pair(0, gate)
    up = take_pair(1, up)
    sig = [jax.nn.sigmoid(v) for v in gate]
    act = [gate[b] * sig[b] for b in range(NC)]
    for b in range(NC):
        keep(0, b, act[b] * up[b])

    def term(a, h):
        cols = pl.ds(h * wide, wide)
        total = None
        for i, w in ((0, 2),) if a == 0 else ((1, 0), (2, 1)):
            for b in range(NC):
                value = nn(acts[i, b], wv[w, b, :, cols])
                total = value if total is None else total + value
        return total

    def to_row(a, h, d):
        there = pl.ds(pl.multiple_of(lax.rem(y + d, NY) * ROW, ROW), ROW)
        return pltpu.make_async_remote_copy(
            src_ref=ys.at[a, h, there], dst_ref=yr.at[a, h, d - 1], send_sem=ry_s.at[a, h, d - 1],
            recv_sem=ry_r.at[a, h, d - 1], device_id=y_dev(d)[0], device_id_type=MESH,
        )

    def split(value):
        pieces = [value[:, k * 128 : (k + 1) * 128].reshape(1, ROW, 128) for k in range(ROW)]
        return jnp.swapaxes(jnp.concatenate(pieces, axis=0), 0, 1)

    def turn_out(value):
        for yy in range(NY):
            sq[:, yy] = split(value[yy * ROW : (yy + 1) * ROW])
        rq[0] = sq[zx]

        def send(d, _):
            there, t = zx_dev(d)
            pltpu.make_async_remote_copy(
                src_ref=sq.at[t], dst_ref=rq.at[d], send_sem=qs_s.at[0], recv_sem=qs_r.at[0],
                device_id=there, device_id_type=MESH,
            ).start()
            return 0

        lax.fori_loop(1, ROW, send, 0)

    def turn_back(d):
        return pltpu.make_async_remote_copy(
            src_ref=uq.at[lax.rem(y + d, NY)], dst_ref=vq.at[d], send_sem=qy_s.at[d - 1],
            recv_sem=qy_r.at[d - 1], device_id=y_dev(d)[0], device_id_type=MESH,
        )

    def turn_sum():
        some = rq.at[pl.ds(1, ROW - 1)]
        pltpu.make_async_copy(some, some, qs_r.at[0]).wait()
        uq[...] = jnp.sum(rq[...].astype(F32), axis=0).astype(BF)
        for d in (2, 1, 3):
            turn_back(d).start()
        vq[0] = uq[y]

    def scatter_first(a, h):
        value = term(a, h)
        if (a, h) == TURN_S:
            turn_out(value.astype(BF))
            return
        mine[a, h] = value
        ys[a, h] = value.astype(BF)
        for d in (2, 1, 3):
            to_row(a, h, d).start()

    def scatter_y(a, h):
        here = pl.ds(pl.multiple_of(y * ROW, ROW), ROW)
        value = mine[a, h, here]
        for d in (1, 3, 2):
            to_row(a, h, d).wait_recv()
            value = value + yr[a, h, d - 1].astype(F32)
        value = value.astype(BF)
        zs[a, h] = split(value)
        zr[a, h, 0] = zs[a, h, zx]

        def send(d, _):
            there, t = zx_dev(d)
            pltpu.make_async_remote_copy(
                src_ref=zs.at[a, h, t], dst_ref=zr.at[a, h, d], send_sem=rz_s.at[a, h],
                recv_sem=rz_r.at[a, h], device_id=there, device_id_type=MESH,
            ).start()
            return 0

        lax.fori_loop(1, ROW, send, 0)

    def scatter_zx(a, h):
        if (a, h) == TURN_S:
            for d in (1, 3, 2):
                turn_back(d).wait_recv()
            total = jnp.sum(vq[...].astype(F32), axis=0).astype(BF)
        else:
            some = zr.at[a, h, pl.ds(1, ROW - 1)]
            pltpu.make_async_copy(some, some, rz_r.at[a, h]).wait()
            total = jnp.sum(zr[a, h].astype(F32), axis=0).astype(BF)
        for k in range(ROW):
            col = h * wide + k * 128
            (out_ref, gin_ref)[a][:, col : col + 128] = total[k : k + 1, :]

    def grad(ref, i, a):
        share_act(i).wait_recv()
        gact[i, c] = acts[i, c]
        both = jnp.concatenate([gact[i, b] for b in range(NC)], axis=0)
        act_value = jnp.transpose(both.astype(F32)).astype(BF)
        for j in range(width // 1024):
            cols = pl.ds(j * 1024, 1024)
            ref[:, cols] = nn(act_value, whole[a, :, cols]).astype(BF)

    scatter_first(0, 0)
    scatter_first(0, 1)
    share_act(0).start()
    dhid = take_pair(2, dhid)
    for b in range(NC):
        keep(1, b, dhid[b] * up[b] * sig[b] * (1.0 + gate[b] * (1.0 - sig[b])))
        keep(2, b, dhid[b] * act[b])
    scatter_first(1, 0)
    scatter_first(1, 1)
    share_act(1).start()
    share_act(2).start()
    scatter_y(0, 0)
    scatter_y(0, 1)
    scatter_y(1, 1)
    turn_sum()
    for a in range(2):
        share(a).wait_recv()
    grad(gd_ref, 0, 1)
    grad(gg_ref, 1, 0)
    grad(gu_ref, 2, 0)
    for a in range(2):
        for h in range(parts):
            scatter_zx(a, h)

    for s in straight:
        some = zxb.at[s, pl.ds(0, ROW - 1)]
        pltpu.make_async_copy(some, some, zx_s.at[s]).wait()
        for d in range(1, NY):
            to_y(s, d).wait_send()
    some = gq.at[0, pl.ds(0, NY - 1)]
    pltpu.make_async_copy(some, some, q_s.at[0]).wait()
    some = gq.at[pl.ds(0, ROW - 1)]
    pltpu.make_async_copy(some, some, q_s.at[1]).wait()
    for i in range(3):
        to_pair(i).wait_send()
        weights(i).wait_send()
        share_act(i).wait_send()
    for a in range(2):
        share(a).wait_send()
    for a in range(2):
        for h in range(parts):
            if (a, h) == TURN_S:
                some = sq.at[pl.ds(0, ROW - 1)]
                pltpu.make_async_copy(some, some, qs_s.at[0]).wait()
                for d in range(1, NY):
                    turn_back(d).wait_send()
                continue
            for d in range(1, NY):
                to_row(a, h, d).wait_send()
            some = zs.at[a, h, pl.ds(0, ROW - 1)]
            pltpu.make_async_copy(some, some, rz_s.at[a, h]).wait()


def store_kernel(*refs):
    sems = refs[-1]
    n = (len(refs) - 1) // 2
    copies = [pltpu.make_async_copy(refs[i], refs[n + i], sems.at[i]) for i in range(n)]
    for copy in copies:
        copy.start()
    for copy in copies:
        copy.wait()


def per_device(tokens, gate_weight, up_weight, down_weight, cotangent):
    units, width = gate_weight.shape
    tokens_all = ROW * NY * NC
    wide = ROW * 128
    parts = width // wide
    st = 2 * parts
    vm = pl.BlockSpec(memory_space=pltpu.VMEM)
    hbm = pl.BlockSpec(memory_space=pltpu.HBM)
    sem = pltpu.SemaphoreType.DMA
    shapes = [jax.ShapeDtypeStruct((1, width), BF)] * 2
    shapes += [jax.ShapeDtypeStruct((units, width), BF)] * 3
    inputs = (tokens, cotangent, gate_weight, up_weight, down_weight)
    results = pl.pallas_call(
        exchange_kernel,
        out_shape=shapes,
        in_specs=[hbm] * 5,
        out_specs=[vm] * 5,
        scratch_shapes=[
            pltpu.VMEM((2, 1, width), BF),
            pltpu.VMEM((3, NC, units, width), BF),
            pltpu.VMEM((2 * width // 128, 128), F32),
            pltpu.VMEM((st, ROW, 128), BF),
            pltpu.VMEM((st, ROW, ROW, 128), BF),
            pltpu.VMEM((2, tokens_all, width), BF),
            pltpu.VMEM((3, NC, HALF, units), BF),
            pltpu.VMEM((3, NC, HALF, units), BF),
            pltpu.VMEM((3, NC, HALF, units), BF),
            pltpu.VMEM((3, NC, HALF, units), BF),
            pltpu.VMEM((2, parts, HALF, wide), F32),
            pltpu.VMEM((2, parts, HALF, wide), BF),
            pltpu.VMEM((2, parts, NY - 1, ROW, wide), BF),
            pltpu.VMEM((2, parts, ROW, ROW, 128), BF),
            pltpu.VMEM((2, parts, ROW, ROW, 128), BF),
            sem((5,)), sem((st,)), sem((st,)), sem((st, NY - 1)), sem((st, NY - 1)),
            sem((3,)), sem((3,)), sem((2,)), sem((2,)), sem((3,)), sem((3,)), sem((3,)), sem((3,)),
            sem((2, parts, NY - 1)), sem((2, parts, NY - 1)),
            sem((2, parts)), sem((2, parts)),
            pltpu.VMEM((ROW, NY, ROW, 128), BF),
            pltpu.VMEM((ROW, NY, ROW, 128), BF),
            pltpu.VMEM((ROW, NY, ROW, 128), BF),
            pltpu.VMEM((NY, ROW, 128), BF),
            pltpu.VMEM((NY, ROW, 128), BF),
            sem((2,)), sem((2,)), sem((1,)), sem((1,)), sem((NY - 1,)), sem((NY - 1,)),
        ],
        compiler_params=pltpu.CompilerParams(
            collective_id=0, has_side_effects=True, vmem_limit_bytes=48 << 20
        ),
        name="exchange",
    )(*[pltpu.with_memory_space_constraint(x, pltpu.HBM) for x in inputs])
    return tuple(
        pl.pallas_call(
            store_kernel,
            out_shape=shapes,
            in_specs=[vm] * 5,
            out_specs=[hbm] * 5,
            scratch_shapes=[sem((5,))],
            compiler_params=pltpu.CompilerParams(vmem_limit_bytes=1 << 20),
            name="store",
        )(*results)
    )


def solution(mesh):
    spec = P(("tok", "wo"), "wi")
    return jax.shard_map(
        per_device, mesh=mesh, in_specs=(spec,) * 5, out_specs=(spec,) * 5, check_vma=False
    )
```
